512 devices in a mesh: section: 2 (over core), chan: 16 (over z), tok: 16 (over y, x).
Axes of the slice: x: 4, y: 4, z: 16, core: 2. Of those that a mesh axis runs over, the one named last changes fastest.
Arguments:
- gate_streams: bfloat16 [2, 2, 8192, 8192], P('section', None, 'chan', 'tok'), may hold values from -6 to 6
- inputs: bfloat16 [8192, 8192], P('chan', 'tok'), may hold values from -6 to 6
- medium_taps: bfloat16 [8192, 128], P('chan'), may hold values from -0.5 to 0.5
- residues: float32 [8192, 16], P('chan'), may hold values from -3 to 3
- decay_rates: float32 [8192, 16], P('chan'), may hold values from 2.3193359e-05 to 0.034, as said below
Outputs:
- mixer_out: bfloat16 [2, 8192, 8192], P('section', 'chan', 'tok')
The draws below stay inside these ranges and needn't reach their ends.
Inputs may be any that keep to these rules, and one draw needn't show every extreme that they name: `decay_rates`: every rate is positive.
All inputs are finite; a program needn't handle non-finite values.
Results may differ from the reference program's by a relative error of at most 0.0057.
Values may be sent and summed in bfloat16 or wider, within the bound.
A program may use at most 64 MiB of HBM per device.

```python
import math
import jax
import jax.numpy as jnp
from jax import lax

D = 8192
MR_LEN = 128
ORDER = 16
SEQ = 8192


def draw_decay_rates(key, part):
    choose_key, slow_key, fast_key = jax.random.split(jax.random.fold_in(key, 7), 3)
    rate_shape = (D, ORDER)
    slow_rates = jnp.exp(jax.random.uniform(slow_key, rate_shape, jnp.float32, jnp.log(0.2 / SEQ), jnp.log(2.0 / SEQ)))
    fast_rates = jnp.exp(jax.random.uniform(fast_key, rate_shape, jnp.float32, jnp.log(1.0 / 50.0), jnp.log(1.0 / 30.0)))
    slow_share = 0.5
    chosen = jax.random.uniform(choose_key, rate_shape, jnp.float32) < slow_share
    return jnp.where(chosen, slow_rates, fast_rates).astype(jnp.float32)


def level_of(own_key, shape, cuts, smallest, top_value):
    gain, own = 1.0, jax.random.fold_in(own_key, 6)
    for dim, shards_of in cuts:
        heights = jnp.exp(jax.random.uniform(jax.random.fold_in(own, dim), (shards_of,), jnp.float32, smallest / len(cuts), top_value / len(cuts)))
        gain = gain * jnp.repeat(heights, shape[dim] // shards_of).reshape([-1 if axis == dim else 1 for axis in range(len(shape))])
    return gain


def noise(stream_key, shape, spread, bound, cuts=(), kind=jnp.bfloat16):
    drawn = spread * jax.random.normal(stream_key, shape, jnp.float32)
    if cuts:
        drawn = drawn * level_of(stream_key, shape, cuts, -0.22, 0.18)
    return jnp.clip(drawn, -bound, bound).astype(kind)


def setup_inputs(seed: int = 0) -> dict:
    arg_keys = jax.random.split(jax.random.key(seed), 6)
    return {
        "gate_streams": noise(arg_keys[0], (2, 2, D, SEQ), 1.0, 6.0, ((0, 2), (2, 16), (3, 16))),
        "inputs": noise(arg_keys[1], (D, SEQ), 1.0, 6.0, ((0, 16), (1, 16))),
        "medium_taps": noise(arg_keys[2], (D, MR_LEN), MR_LEN ** -0.5, 0.5, ((0, 16),)),
        "residues": noise(arg_keys[3], (D, ORDER), 0.5, 3.0, ((0, 16),), jnp.float32),
        "decay_rates": draw_decay_rates(jax.random.fold_in(arg_keys[5], 71), 0),
    }


def medium_filter(product, medium_taps):
    padded = jnp.pad(product.astype(jnp.float32), ((0, 0), (MR_LEN - 1, 0)))
    taps_wide = medium_taps.astype(jnp.float32)
    summed = jnp.zeros(product.shape, jnp.float32)
    for offset in range(MR_LEN):
        begin = MR_LEN - 1 - offset
        summed = summed + taps_wide[:, offset:offset + 1] * padded[:, begin:begin + SEQ]
    return summed

def long_convolve(gated_signal, residues, decay_rates):
    scaled = residues * jnp.sqrt(1.0 - jnp.exp(-2.0 * decay_rates))
    positions = jnp.arange(SEQ).astype(jnp.float32)
    long_taps = lax.optimization_barrier(jnp.sum(scaled[:, :, None] * jnp.exp(-decay_rates[:, :, None] * positions[None, None, :]), axis=1))
    length = 2 * SEQ
    spectrum = jnp.fft.rfft(gated_signal.astype(jnp.float32), n=length, axis=1) * jnp.fft.rfft(long_taps, n=length, axis=1)
    return jnp.fft.irfft(spectrum, n=length, axis=1)[:, :SEQ]

def reference(gate_streams, inputs, medium_taps, residues, decay_rates):
    channel_group = math.gcd(D, 64)
    groups_count = D // channel_group

    def grouped(array):
        return array.reshape(groups_count, channel_group, array.shape[-1])
    product = (gate_streams[0, 1].astype(jnp.float32) * inputs.astype(jnp.float32)).astype(jnp.bfloat16)
    medium = lax.map(lambda members: medium_filter(members[0], members[1]), (grouped(product), grouped(medium_taps))).reshape(D, SEQ)
    gated_medium = (gate_streams[0, 0].astype(jnp.float32) * medium).astype(jnp.bfloat16)
    stream = inputs.astype(jnp.float32) + gated_medium.astype(jnp.float32)
    gated_signal = (gate_streams[1, 1].astype(jnp.float32) * stream).astype(jnp.bfloat16)
    long_out = lax.map(lambda members: long_convolve(members[0], members[1], members[2]), (grouped(gated_signal), grouped(residues), grouped(decay_rates))).reshape(D, SEQ)
    mixed_long = (stream + gate_streams[1, 0].astype(jnp.float32) * long_out).astype(jnp.bfloat16)
    return jnp.stack([gated_medium, mixed_long])
```

```python
import jax
import jax.numpy as jnp
import numpy as np
import ml_dtypes
from jax import lax
from jax.experimental import pallas as pl
from jax.experimental.pallas import tpu as pltpu
from jax.sharding import PartitionSpec as P

MESH = pl.DeviceIdType.MESH
f32 = jnp.float32
bf16 = jnp.bfloat16
BLK = 128
NT = (((1,), (1,)), ((), ()))


def split_np(a):
    hi = a.astype(ml_dtypes.bfloat16)
    lo = (a - hi.astype(np.float64)).astype(ml_dtypes.bfloat16)
    return hi, lo


def tables():
    n = 2 * BLK
    omega = 2.0 * np.pi * (np.arange(BLK) + 0.5) / n
    m = np.arange(n)
    angle = m[:, None] * omega[None, :]
    forward = np.concatenate([np.cos(angle), -np.sin(angle)], axis=1)
    inverse = forward.T / BLK
    f_hi, f_lo = split_np(forward)
    late_hi, late_lo = split_np(inverse[:, BLK:])
    ft_hi, ft_lo = split_np(forward[:BLK].T)
    gt_hi, gt_lo = split_np(inverse[:, :BLK].T)
    eye = np.eye(BLK).astype(ml_dtypes.bfloat16)
    wide = np.concatenate([f_hi, f_lo, gt_hi, gt_lo], axis=0)
    narrow = np.concatenate([late_hi, late_lo, ft_hi, ft_lo, eye, eye[::-1]], axis=0)
    return wide, narrow


def dot(a, b):
    return jnp.dot(a, b, preferred_element_type=f32)


def dot_nt(a, b):
    return lax.dot_general(a, b, NT, preferred_element_type=f32)


def split(a):
    hi = a.astype(bf16)
    return hi, (a - hi.astype(f32)).astype(bf16)


def kernel(
    gates, x_hbm, taps_hbm, res_hbm, rate_hbm, wide_hbm, narrow_hbm, out,
    g, x, taps, res, rate, wide, narrow, prod, g0, hmed, gm, par, powers, hlong, base, gout, st, send, recv,
    load_sem, pair_send, pair_recv, gm_send, gm_recv, halo_send, halo_recv, st_send, st_recv,
):
    sec = lax.axis_index("section")
    tok = lax.axis_index("tok")
    toks = lax.axis_size("tok")
    chans, cols = x.shape
    nblk = cols // BLK
    tiles = chans // BLK
    order = res.shape[0]
    last = cols - BLK

    def col(b):
        return pl.ds(pl.multiple_of(b * BLK, BLK), BLK)

    tail = pl.ds(last, BLK)
    head = pl.ds(0, last)
    g_tail = pltpu.make_async_copy(gates.at[0, :, :, tail], g.at[:, :, tail], load_sem.at[0])
    x_tail = pltpu.make_async_copy(x_hbm.at[:, tail], x.at[:, tail], load_sem.at[1])
    g_head = pltpu.make_async_copy(gates.at[0, :, :, head], g.at[:, :, head], load_sem.at[2])
    x_head = pltpu.make_async_copy(x_hbm.at[:, head], x.at[:, head], load_sem.at[3])
    l_taps = pltpu.make_async_copy(taps_hbm, taps, load_sem.at[4])
    l_wide = pltpu.make_async_copy(wide_hbm, wide, load_sem.at[5])
    l_narrow = pltpu.make_async_copy(narrow_hbm, narrow, load_sem.at[6])
    l_res = pltpu.make_async_copy(res_hbm, res, load_sem.at[7])
    l_rate = pltpu.make_async_copy(rate_hbm, rate, load_sem.at[8])
    for c in (l_rate, l_res, g_tail, x_tail, x_head, g_head, l_wide, l_narrow, l_taps):
        c.start()

    barrier = pltpu.get_barrier_semaphore()
    pl.semaphore_signal(barrier, inc=1, device_id={"section": 1 - sec}, device_id_type=MESH)

    @pl.when(sec == 1)
    def _():
        @pl.when(tok > 0)
        def _():
            pl.semaphore_signal(barrier, inc=1, device_id={"section": 0, "tok": tok - 1}, device_id_type=MESH)

        def greet(i, carry):
            pl.semaphore_signal(barrier, inc=1, device_id={"tok": i}, device_id_type=MESH)
            return carry

        lax.fori_loop(0, tok, greet, 0)

    halo = pltpu.make_async_remote_copy(
        src_ref=prod.at[:, pl.ds(cols, BLK)], dst_ref=prod.at[:, pl.ds(0, BLK)],
        send_sem=halo_send, recv_sem=halo_recv,
        device_id={"section": 1, "tok": jnp.minimum(tok + 1, toks - 1)}, device_id_type=MESH,
    )
    gates0 = pltpu.make_async_remote_copy(
        src_ref=gates.at[0, :, :, pl.ds(0, BLK)], dst_ref=g0,
        send_sem=pair_send, recv_sem=pair_recv,
        device_id={"section": 1 - sec}, device_id_type=MESH,
    )

    def gm_copy(b):
        return pltpu.make_async_remote_copy(
            src_ref=gm.at[b], dst_ref=gm.at[b],
            send_sem=gm_send.at[b], recv_sem=gm_recv.at[b],
            device_id={"section": 1 - sec}, device_id_type=MESH,
        )

    def product(gate, values):
        return (gate.astype(f32) * values.astype(f32)).astype(bf16)

    rows_step = min(256, chans)
    f_hi = wide.at[pl.ds(0, 2 * BLK), :]
    f_lo = wide.at[pl.ds(2 * BLK, 2 * BLK), :]
    gt_hi = wide.at[pl.ds(4 * BLK, BLK), :]
    gt_lo = wide.at[pl.ds(5 * BLK, BLK), :]
    late_hi = narrow.at[pl.ds(0, 2 * BLK), :]
    late_lo = narrow.at[pl.ds(2 * BLK, 2 * BLK), :]
    ft_hi = narrow.at[pl.ds(4 * BLK, 2 * BLK), :]
    ft_lo = narrow.at[pl.ds(6 * BLK, 2 * BLK), :]
    eye = narrow.at[pl.ds(8 * BLK, BLK), :]
    flip = narrow.at[pl.ds(9 * BLK, BLK), :]

    def medium_taps():
        for r in range(0, chans, rows_step):
            rows = pl.ds(r, rows_step)
            hmed[rows, :] = dot(taps[rows, :], wide[pl.ds(0, BLK), :]) + dot(
                taps[rows, :], wide[pl.ds(2 * BLK, BLK), :]
            )

    def medium_block(start, gate_of, b):
        for r in range(0, chans, rows_step):
            rows = pl.ds(r, rows_step)
            window = prod[rows, pl.ds(start, 2 * BLK)]
            spec = dot(window, f_hi[...]) + dot(window, f_lo[...])
            xr, xi = spec[:, :BLK], spec[:, BLK:]
            hr, hi = hmed[rows, :BLK], hmed[rows, BLK:]
            y = jnp.concatenate([xr * hr - xi * hi, xr * hi + xi * hr], axis=1)
            y_hi, y_lo = split(y)
            value = dot(y_hi, late_hi[...]) + (dot(y_lo, late_hi[...]) + dot(y_hi, late_lo[...]))
            gm[b, rows, :] = (gate_of(rows) * value).astype(bf16)

    @pl.when(sec == 0)
    def _():
        g_tail.wait()
        x_tail.wait()
        prod[:, pl.ds(cols, BLK)] = product(g[1, :, tail], x[:, tail])
        pl.semaphore_wait(barrier, 1 + jnp.where(tok < toks - 1, 1, 0))

        @pl.when(tok < toks - 1)
        def _():
            halo.start()

        gates0.start()
        x_head.wait()
        g_head.wait()
        prod[:, pl.ds(BLK, last)] = product(g[1, :, head], x[:, head])
        l_taps.wait()
        l_wide.wait()
        l_narrow.wait()
        medium_taps()

        def step(b, carry):
            medium_block(
                pl.multiple_of(b * BLK, BLK), lambda rows: g[0, rows, col(b)].astype(f32), b
            )
            gm_copy(b).start()
            out[:, col(b)] = gm[b]
            return carry

        lax.fori_loop(1, nblk, step, 0)
        gm_copy(0).wait_recv()
        out[:, pl.ds(0, BLK)] = gm[0]
        l_res.wait()
        l_rate.wait()

        @pl.when(tok < toks - 1)
        def _():
            halo.wait_send()

        gates0.wait_send()
        for b in range(1, nblk):
            gm_copy(b).wait_send()

    def prepare():
        for c in range(tiles):
            lanes = pl.ds(c * BLK, BLK)
            r = rate[:, lanes]
            scaled = res[:, lanes] * jnp.sqrt(1.0 - jnp.exp(-2.0 * r))
            par[0, c] = r
            par[1, c] = scaled * jnp.exp(-r)
            par[2, c] = jnp.exp(-float(BLK) * r)
            par[3, c] = jnp.exp(-float(cols) * r)
            offsets = lax.broadcasted_iota(jnp.int32, (8, BLK), 0).astype(f32)
            e8 = jnp.exp(-8.0 * r)
            first = jnp.zeros((BLK, BLK), f32)
            steps = {}
            for width in (8, 16, 32, 64):
                steps[width] = jnp.exp(-float(width) * r)
            for n in range(order):
                p = jnp.exp(-r[n : n + 1, :] * offsets)
                for width in (8, 16, 32, 64):
                    p = jnp.concatenate([p, p * steps[width][n : n + 1, :]], axis=0)
                powers[c, n] = p
                first = first + scaled[n : n + 1, :] * p
            t_hi, t_lo = split(first)
            hlong[c] = dot(ft_hi[...], t_hi) + (dot(ft_hi[...], t_lo) + dot(ft_lo[...], t_hi))

    def turn(block):
        return dot_nt(eye[...], block)

    def block_states(b):
        us = []
        for c in range(tiles):
            rows = pl.ds(c * BLK, BLK)
            stream = turn(x[rows, col(b)]) + turn(gm[b, rows, :])
            u = (turn(g[1, rows, col(b)]) * stream).astype(bf16)
            base[c, b] = stream
            back = dot(flip[...], u)
            parts = [jnp.sum(powers[c, n] * back, axis=0, keepdims=True) for n in range(order)]
            st[c, b] = jnp.concatenate(parts, axis=0)
            us.append(u)
        return us

    def block_within(b, us):
        for c in range(tiles):
            rows = pl.ds(c * BLK, BLK)
            u = us[c]
            spec = dot(ft_hi[...], u) + dot(ft_lo[...], u)
            xr, xi = spec[:BLK], spec[BLK:]
            hr, hi = hlong[c, :BLK], hlong[c, BLK:]
            y = jnp.concatenate([xr * hr - xi * hi, xr * hi + xi * hr], axis=0)
            y_hi, y_lo = split(y)
            value = dot(gt_hi[...], y_hi) + (dot(gt_hi[...], y_lo) + dot(gt_lo[...], y_hi))
            gate = turn(g[0, rows, col(b)])
            gout[c, b] = gate
            base[c, b] = base[c, b] + gate * value

    def st_copy(target):
        return pltpu.make_async_remote_copy(
            src_ref=send, dst_ref=recv.at[tok],
            send_sem=st_send.at[target], recv_sem=st_recv.at[tok],
            device_id={"tok": target}, device_id_type=MESH,
        )

    @pl.when(sec == 1)
    def _():
        l_rate.wait()
        l_res.wait()
        l_narrow.wait()
        prepare()
        l_taps.wait()
        l_wide.wait()
        medium_taps()
        x_tail.wait()
        x_head.wait()
        g_tail.wait()
        g_head.wait()

        @pl.when(tok == 0)
        def _():
            prod[:, pl.ds(0, BLK)] = jnp.zeros((chans, BLK), bf16)

        gates0.wait_recv()
        prod[:, pl.ds(BLK, BLK)] = product(g0[1], x[:, pl.ds(0, BLK)])
        pl.semaphore_wait(barrier, toks - tok)

        def step(b, carry):
            gm_copy(b).wait_recv()
            block_within(b, block_states(b))
            return carry

        lax.fori_loop(1, nblk, step, 0)

        @pl.when(tok > 0)
        def _():
            halo.wait_recv()

        medium_block(0, lambda rows: g0[0, rows, :].astype(f32), 0)
        gm_copy(0).start()
        us = block_states(0)
        for c in range(tiles):
            end = st[c, 0]
            for b in range(1, nblk):
                end = end * par[2, c] + st[c, b]
            send[c] = end

        def give(target, carry):
            st_copy(target).start()
            return carry

        lax.fori_loop(tok + 1, toks, give, 0)
        block_within(0, us)

        def take(source, entering):
            pltpu.make_async_remote_copy(
                src_ref=send, dst_ref=recv.at[source],
                send_sem=st_send.at[source], recv_sem=st_recv.at[source],
                device_id={"tok": source}, device_id_type=MESH,
            ).wait_recv()
            return entering * par[3] + recv[source]

        entering = lax.fori_loop(0, tok, take, jnp.zeros((tiles, order, BLK), f32))
        send_w = []
        for b in range(nblk):
            send_w.append(entering * par[1])
            entering = entering * par[2] + st[:, b]
        half = BLK // 2
        for c in range(tiles):
            rows = pl.ds(c * BLK, BLK)
            totals = [[] for _ in range(nblk)]
            for part in range(2):
                lines = pl.ds(part * half, half)
                acc = [jnp.zeros((half, BLK), f32) for _ in range(nblk)]
                for n in range(order):
                    p = powers[c, n, lines, :]
                    for b in range(nblk):
                        acc[b] = acc[b] + p * send_w[b][c, n : n + 1, :]
                for b in range(nblk):
                    totals[b].append((base[c, b, lines, :] + gout[c, b, lines, :] * acc[b]).astype(bf16))
            for b in range(nblk):
                mixed = jnp.concatenate(totals[b], axis=0)
                out[rows, pl.ds(b * BLK, BLK)] = turn(mixed).astype(bf16)

        def finish(target, carry):
            st_copy(target).wait_send()
            return carry

        lax.fori_loop(tok + 1, toks, finish, 0)
        gm_copy(0).wait_send()


def on_device(gate_streams, inputs, medium_taps, residues, decay_rates):
    wide, narrow = (jnp.asarray(a) for a in tables())
    chans, cols = inputs.shape
    order = residues.shape[1]
    toks = lax.axis_size("tok")
    tiles, nblk = chans // BLK, cols // BLK
    hbm = pl.BlockSpec(memory_space=pltpu.HBM)
    dma = pltpu.SemaphoreType.DMA
    result = pl.pallas_call(
        kernel,
        out_shape=jax.ShapeDtypeStruct((chans, cols), bf16),
        in_specs=[hbm] * 7,
        out_specs=pl.BlockSpec(memory_space=pltpu.VMEM),
        scratch_shapes=[
            pltpu.VMEM((2, chans, cols), bf16),
            pltpu.VMEM((chans, cols), bf16),
            pltpu.VMEM(medium_taps.shape, bf16),
            pltpu.VMEM((order, chans), f32),
            pltpu.VMEM((order, chans), f32),
            pltpu.VMEM(wide.shape, bf16),
            pltpu.VMEM(narrow.shape, bf16),
            pltpu.VMEM((chans, cols + BLK), bf16),
            pltpu.VMEM((2, chans, BLK), bf16),
            pltpu.VMEM((chans, 2 * BLK), f32),
            pltpu.VMEM((nblk, chans, BLK), bf16),
            pltpu.VMEM((4, tiles, order, BLK), f32),
            pltpu.VMEM((tiles, order, BLK, BLK), f32),
            pltpu.VMEM((tiles, 2 * BLK, BLK), f32),
            pltpu.VMEM((tiles, nblk, BLK, BLK), f32),
            pltpu.VMEM((tiles, nblk, BLK, BLK), f32),
            pltpu.VMEM((tiles, nblk, order, BLK), f32),
            pltpu.VMEM((tiles, order, BLK), f32),
            pltpu.VMEM((toks, tiles, order, BLK), f32),
            dma((9,)),
            dma,
            dma,
            dma((nblk,)),
            dma((nblk,)),
            dma,
            dma,
            dma((toks,)),
            dma((toks,)),
        ],
        compiler_params=pltpu.CompilerParams(
            collective_id=0, has_side_effects=True, vmem_limit_bytes=62 * 1024 * 1024
        ),
    )(gate_streams, inputs, medium_taps, residues.T, decay_rates.T, wide, narrow)
    return result[None]


def solution(mesh):
    placed = (
        P("section", None, "chan", "tok"),
        P("chan", "tok"),
        P("chan", None),
        P("chan", None),
        P("chan", None),
    )
    return jax.shard_map(
        on_device,
        mesh=mesh,
        in_specs=placed,
        out_specs=P("section", "chan", "tok"),
        check_vma=False,
    )
```
